32 devices in a mesh: row: 4 (over x, core), col: 8 (over z, y).
Axes of the slice: x: 2, y: 2, z: 4, core: 2. Of those that a mesh axis runs over, the one named last changes fastest.
Arguments:
- features: bfloat16 [4096, 256], P(('row', 'col')), may hold values from -6 to 6
- weight: bfloat16 [256, 256], replicated, may hold values from -0.375 to 0.375
- bias_vector: float32 [256], replicated, may hold values from -3 to 3
- out_grad: bfloat16 [4096, 256], P(('row', 'col')), may hold values from -6 to 6
- adj_tiles: bfloat16 [4, 8, 96, 128, 128], P('row', 'col'), as said below
- tile_pos: int32 [4, 8, 96], P('row', 'col'), may hold values from 0 to 31
- tile_count: int32 [4, 8], P('row', 'col'), may hold values from 24 to 96, as said below
Outputs:
- hidden_out: bfloat16 [4096, 256], P(('row', 'col'))
- feature_grad: bfloat16 [4096, 256], P(('row', 'col'))
- weight_grad: float32 [256, 256], replicated
- bias_grad: float32 [256], replicated
The draws below stay inside these ranges and needn't reach their ends.
Inputs may be any that keep to these rules, and one draw needn't show every extreme that they name: `tile_pos`: several slots of one grid position may name the same tile position; their tiles add. Only the first tile_count slots of a grid position are live. In every draw some grid position has exactly 96 live slots and some other one the least number. `adj_tiles`: entries are nonnegative edge weights.
All inputs are finite; a program needn't handle non-finite values.
Results may differ from the reference program's by a relative error of at most 0.018.
Values may be sent and summed in bfloat16 or wider, within the bound.
No kernel may reach another device: no remote copies, remote signals or barrier semaphores. Data moves between devices by JAX's collectives and lax.ppermute only.
A program may use at most 64 MiB of HBM per device.

```python
import math
import jax
import jax.numpy as jnp
from jax import lax

F = 256
TILE = 128
ROWS_DEV = 128
TILES_DEV = 96
NODES = 4096
N_ROW = 4
N_COL = 8


def draw_adj_tiles(key, part):
    key = jax.random.fold_in(key, 5)
    height = 2.2 * math.sqrt(ROWS_DEV / TILES_DEV) / TILE
    uniform_vals = jax.random.uniform(key, (N_ROW, N_COL, TILES_DEV, TILE, TILE), jnp.float32)
    values = height * uniform_vals
    return values.astype(jnp.bfloat16)


def draw_tile_count(key, part):
    key = jax.random.fold_in(key, 7)
    first_key, second_key = jax.random.split(key)
    lowest = max(TILES_DEV // 4, 1)
    counts = jax.random.randint(first_key, (N_ROW * N_COL,), lowest, TILES_DEV + 1, dtype=jnp.int32)
    shuffled = jax.random.permutation(second_key, N_ROW * N_COL)
    counts = counts.at[shuffled[0]].set(TILES_DEV)
    counts = counts.at[shuffled[1]].set(lowest)
    return counts.reshape(N_ROW, N_COL).astype(jnp.int32)


def set_ends(values, stream_key, least, top_value):
    index_at = [jax.random.randint(jax.random.fold_in(stream_key, axis), (), 0, length) for axis, length in enumerate(values.shape)]
    longest = values.shape.index(max(values.shape))
    next_to = index_at[:longest] + [(index_at[longest] + 1) % values.shape[longest]] + index_at[longest + 1:]
    return values.at[tuple(index_at)].set(least).at[tuple(next_to)].set(top_value)


def block_scale(rng, dims, shards, smallest, largest):
    loudness = 1.0
    for position, parts in shards:
        heights = jax.random.uniform(jax.random.fold_in(jax.random.fold_in(rng, 6), position), (parts,), jnp.float32, smallest / len(shards), largest / len(shards))
        loudness = loudness * jnp.repeat(jnp.exp(heights), dims[position] // parts).reshape((-1,) + (1,) * (len(dims) - 1 - position))
    return loudness


def normal_values(rng, extent, deviation, limit, cuts=(), kind=jnp.bfloat16):
    gain = block_scale(rng, extent, cuts, -0.22, 0.18) if cuts else 1.0
    entries = jax.random.normal(rng, extent, jnp.float32) * deviation * gain
    return jnp.minimum(jnp.maximum(entries, -limit), limit).astype(kind)


def setup_inputs(seed: int = 0) -> dict:
    streams_of = jax.random.split(jax.random.key(seed), 8)
    features = normal_values(streams_of[0], (NODES, F), 1.0, 6.0, ((0, 32),))
    weight = normal_values(streams_of[1], (F, F), F ** -0.5, 0.375)
    bias_vector = normal_values(streams_of[2], (F,), 0.5, 3.0, (), jnp.float32)
    out_grad = normal_values(streams_of[3], (NODES, F), 1.0, 6.0, ((0, 32),))
    adj_tiles = draw_adj_tiles(jax.random.fold_in(streams_of[7], 71), 0)
    tile_pos = set_ends(jax.random.randint(streams_of[5], (N_ROW, N_COL, TILES_DEV), 0, N_ROW * N_COL * (ROWS_DEV // TILE) ** 2), jax.random.fold_in(streams_of[5], 1), 0, (N_ROW * N_COL * (ROWS_DEV // TILE) ** 2) - 1).astype(jnp.int32)
    tile_count = draw_tile_count(jax.random.fold_in(streams_of[7], 71), 0)
    return {"features": features, "weight": weight, "bias_vector": bias_vector, "out_grad": out_grad, "adj_tiles": adj_tiles, "tile_pos": tile_pos, "tile_count": tile_count}


def reference(features, weight, bias_vector, out_grad, adj_tiles, tile_pos, tile_count):
    row_tiles = N_COL * ROWS_DEV // TILE
    col_tiles = N_ROW * ROWS_DEV // TILE
    grid_size = N_ROW * N_COL
    feat_blocks = features.reshape(N_ROW, N_COL, ROWS_DEV, F)
    flat_tiles = adj_tiles.reshape(grid_size, TILES_DEV, TILE, TILE)
    flat_pos = tile_pos.reshape(grid_size, TILES_DEV)
    flat_count = tile_count.reshape(grid_size)
    slot_index = jnp.arange(TILES_DEV, dtype=jnp.int32)
    flat_index = jnp.arange(grid_size, dtype=jnp.int32)

    def forward_one(totals, inputs):
        grid_index, tile_set, positions, live_count = inputs
        row_index = grid_index // N_COL
        col_index = grid_index % N_COL
        sources = lax.dynamic_index_in_dim(feat_blocks, col_index, 1, keepdims=False)
        sources = sources.reshape(col_tiles, TILE, F)
        picked = sources[positions % col_tiles]
        product = jnp.einsum('tij,tjf->tif', tile_set.astype(jnp.float32), picked.astype(jnp.float32))
        product = jnp.where((slot_index < live_count)[:, None, None], product, jnp.float32(0.0))
        partial_value = jax.ops.segment_sum(product, positions // col_tiles, num_segments=row_tiles)
        partial_value = partial_value.reshape(N_COL * ROWS_DEV, F).astype(jnp.bfloat16)
        partial_value = lax.optimization_barrier(partial_value).astype(jnp.float32)
        current = lax.dynamic_index_in_dim(totals, row_index, 0, keepdims=False)
        totals = lax.dynamic_update_index_in_dim(totals, current + partial_value, row_index, 0)
        return (totals, None)
    start_totals = jnp.zeros((N_ROW, N_COL * ROWS_DEV, F), jnp.float32)
    totals, _ = lax.scan(forward_one, start_totals, (flat_index, flat_tiles, flat_pos, flat_count))
    aggregated = totals.reshape(NODES, F).astype(jnp.bfloat16)
    pre = jnp.dot(aggregated, weight, preferred_element_type=jnp.float32) + bias_vector
    gate_value = jax.nn.sigmoid(pre)
    hidden_out = (pre * gate_value).astype(jnp.bfloat16)
    pre_grad = (out_grad.astype(jnp.float32) * (gate_value * (1.0 + pre * (1.0 - gate_value)))).astype(jnp.bfloat16)
    grad_scale = 1.0 / math.sqrt(NODES)
    weight_grad = jnp.dot(aggregated.T, pre_grad, preferred_element_type=jnp.float32) * grad_scale
    bias_grad = lax.optimization_barrier(jnp.sum(pre_grad.astype(jnp.float32), axis=0)) * grad_scale
    agg_grad = jnp.dot(pre_grad, weight.T, preferred_element_type=jnp.float32).astype(jnp.bfloat16)
    panels = agg_grad.reshape(N_ROW, row_tiles, TILE, F)

    def backward_one(totals, inputs):
        grid_index, tile_set, positions, live_count = inputs
        row_index = grid_index // N_COL
        col_index = grid_index % N_COL
        row_src = lax.dynamic_index_in_dim(panels, row_index, 0, keepdims=False)
        picked = row_src[positions // col_tiles]
        product = jnp.einsum('tji,tjf->tif', tile_set.astype(jnp.float32), picked.astype(jnp.float32))
        product = jnp.where((slot_index < live_count)[:, None, None], product, jnp.float32(0.0))
        column_terms = jax.ops.segment_sum(product, positions % col_tiles, num_segments=col_tiles)
        column_terms = column_terms.reshape(N_ROW, ROWS_DEV, F)
        current = lax.dynamic_index_in_dim(totals, col_index, 1, keepdims=False)
        totals = lax.dynamic_update_index_in_dim(totals, current + column_terms, col_index, 1)
        return (totals, None)
    grad_totals = jnp.zeros((N_ROW, N_COL, ROWS_DEV, F), jnp.float32)
    grad_totals, _ = lax.scan(backward_one, grad_totals, (flat_index, flat_tiles, flat_pos, flat_count))
    feature_grad = grad_totals.reshape(NODES, F).astype(jnp.bfloat16)
    return (hidden_out, feature_grad, weight_grad, bias_grad)
```

```python
import functools
import math

import jax
import jax.numpy as jnp
from jax import lax
from jax.experimental import pallas as pl
from jax.experimental.pallas import tpu as pltpu
from jax.sharding import PartitionSpec as P

BF16 = jnp.bfloat16
F32 = jnp.float32
CHUNK = 8
BIAS_ROWS = 16
VMEM = pl.BlockSpec(memory_space=pltpu.VMEM)
ANY = pl.BlockSpec(memory_space=pl.ANY)
SMEM = pl.BlockSpec(memory_space=pltpu.SMEM)


def swapped(block, axis, bit):
    n = lax.axis_size(axis)
    return lax.ppermute(block, axis, [(i, i ^ bit) for i in range(n)])


def params(mib=32):
    return pltpu.CompilerParams(vmem_limit_bytes=mib * 1024 * 1024)


def build_kernel(col_tiles, pos_ref, count_ref, tiles_ref, panel_ref, stage, acc, sems):
    slots = tiles_ref.shape[0]
    size = tiles_ref.shape[1]
    count = count_ref[0]
    chunks = slots // CHUNK

    def copy(chunk):
        part = pl.ds(chunk * CHUNK, CHUNK)
        return pltpu.make_async_copy(tiles_ref.at[part], stage.at[part], sems.at[chunk])

    for chunk in range(chunks):
        @pl.when(chunk * CHUNK < count)
        def _():
            copy(chunk).start()

    acc[...] = jnp.zeros_like(acc)
    for chunk in range(chunks):
        @pl.when(chunk * CHUNK < count)
        def _():
            copy(chunk).wait()

            def add(slot, carry):
                place = pos_ref[slot]
                acc[place] += stage[slot].astype(F32)
                return carry

            lax.fori_loop(chunk * CHUNK, jnp.minimum(count, (chunk + 1) * CHUNK), add, 0)
    for place in range(acc.shape[0]):
        r, c = place // col_tiles, place % col_tiles
        panel_ref[r * size:(r + 1) * size, c * size:(c + 1) * size] = acc[place].astype(BF16)


def build_panel(positions, count, tiles, row_tiles, col_tiles):
    slots, size = tiles.shape[0], tiles.shape[1]
    places = row_tiles * col_tiles
    return pl.pallas_call(
        functools.partial(build_kernel, col_tiles),
        out_shape=jax.ShapeDtypeStruct((row_tiles * size, col_tiles * size), BF16),
        in_specs=[SMEM, SMEM, ANY],
        out_specs=VMEM,
        scratch_shapes=[
            pltpu.VMEM((slots, size, size), BF16),
            pltpu.VMEM((places, size, size), F32),
            pltpu.SemaphoreType.DMA((slots // CHUNK,)),
        ],
        compiler_params=params(max(52, (slots * 2 + places * 6) * size * size // 2**20 + 4)),
        cost_estimate=pl.CostEstimate(
            flops=slots * size * size, bytes_accessed=2 * slots * size * size, transcendentals=0
        ),
        name="build_panel",
    )(positions, count, tiles)


def peers(count):
    return sorted(range(2, count, 2), key=lambda d: (abs(d - count // 2 - 0.5), d)) + [0]


def tree_order(count):
    return list(range(2, count, 2))


def forward_kernel(count, me_ref, panel_ref, *refs):
    blocks, outs, gathered = refs[:count], refs[count:-1], refs[-1]
    rows = blocks[0].shape[0]
    row_me, col_me = me_ref[0], me_ref[1]
    half = len(outs) // 2
    keeps, sends = outs[:half], outs[half:]
    for d in range(count):
        source = jnp.bitwise_xor(row_me, d)
        gathered[pl.ds(pl.multiple_of(source * rows, rows), rows), :] = blocks[d][...]

    def product(target):
        part = panel_ref[pl.ds(pl.multiple_of(target * rows, rows), rows), :]
        return jnp.dot(part, gathered[...], preferred_element_type=F32)

    for k, d in enumerate(peers(len(outs))):
        sends[k][...] = product(jnp.bitwise_xor(col_me, d + 1)).astype(BF16)
    for k, d in enumerate(peers(len(outs))):
        keeps[k][...] = product(jnp.bitwise_xor(col_me, d))


def forward(me, panel, blocks, col_count):
    rows, width = blocks[0].shape
    half = col_count // 2
    out = pl.pallas_call(
        functools.partial(forward_kernel, len(blocks)),
        out_shape=[jax.ShapeDtypeStruct((rows, width), F32)] * half
        + [jax.ShapeDtypeStruct((rows, width), BF16)] * half,
        in_specs=[SMEM, VMEM] + [VMEM] * len(blocks),
        out_specs=[VMEM] * col_count,
        scratch_shapes=[pltpu.VMEM((rows * len(blocks), width), BF16)],
        compiler_params=params(),
        name="forward_partial",
    )(me, panel, *blocks)
    return out[:half], out[half:]


def split_bias(value):
    high = value.astype(BF16)
    low = (value - high.astype(F32)).astype(BF16)
    return high, low


def bias_rows(value):
    high, low = split_bias(value)
    row = lax.broadcasted_iota(jnp.int32, (BIAS_ROWS, value.shape[1]), 0)
    high, low = high.astype(F32), low.astype(F32)
    return jnp.where(row == 0, high, jnp.where(row == 1, low, 0.0)).astype(BF16)


def bias_value(rows):
    return jnp.sum(rows.astype(F32), axis=0, keepdims=True)


def dense_kernel(count, me_ref, weight_ref, bias_ref, grad_ref, *refs):
    parts, outs = refs[:count], refs[count:]
    hidden_ref, agg_grad_ref, own_ref = outs[:3]
    messages, weights = outs[3:-1], outs[-1]
    rows, width = grad_ref.shape
    groups = len(messages) + 1
    chunk = width // groups
    total = parts[0][...].astype(F32)
    for part in parts[1:]:
        total = total + part[...].astype(F32)
    aggregated = total.astype(BF16)
    weight = weight_ref[...]
    pre = jnp.dot(aggregated, weight, preferred_element_type=F32) + bias_ref[...]
    gate = jax.nn.sigmoid(pre)
    hidden_ref[...] = (pre * gate).astype(BF16)
    pre_grad = (grad_ref[...].astype(F32) * (gate * (1.0 + pre * (1.0 - gate)))).astype(BF16)
    agg_grad = lax.dot_general(
        pre_grad, weight, (((1,), (1,)), ((), ())), preferred_element_type=F32
    ).astype(BF16)
    agg_grad_ref[...] = agg_grad
    weights[...] = lax.dot_general(
        aggregated, pre_grad, (((0,), (0,)), ((), ())), preferred_element_type=F32
    ).astype(BF16)
    bias_part = bias_rows(jnp.sum(pre_grad.astype(F32), axis=0, keepdims=True))

    def section(d):
        group = jnp.right_shift(jnp.bitwise_xor(me_ref[1], d), 1)
        return weights[pl.ds(pl.multiple_of(group * chunk, chunk), chunk), :]

    for d, message in zip(peers(2 * groups)[:-1], messages):
        message[:rows, :] = agg_grad
        message[rows:rows + chunk, :] = section(d)
        message[rows + chunk:, :] = bias_part
    own_ref[:chunk, :] = section(0)
    own_ref[chunk:, :] = bias_part


def dense(me, weight, bias_vector, out_grad, parts, groups):
    rows, width = out_grad.shape
    extra = width // groups + BIAS_ROWS
    return pl.pallas_call(
        functools.partial(dense_kernel, len(parts)),
        out_shape=[jax.ShapeDtypeStruct(out_grad.shape, BF16)] * 2
        + [jax.ShapeDtypeStruct((extra, width), BF16)]
        + [jax.ShapeDtypeStruct((rows + extra, width), BF16)] * (groups - 1),
        in_specs=[SMEM] + [VMEM] * (3 + len(parts)),
        out_specs=[VMEM] * (2 + groups),
        scratch_shapes=[pltpu.VMEM(weight.shape, BF16)],
        compiler_params=params(),
        name="dense_stage",
    )(me, weight, bias_vector, out_grad, *parts)


def tree_sum(values):
    while len(values) > 1:
        values = [values[k] + values[k + 1] for k in range(0, len(values), 2)]
    return values[0]


def gradient_sums(refs, start):
    weight = tree_sum([ref[start(ref):ref.shape[0] - BIAS_ROWS, :].astype(F32) for ref in refs])
    bias = tree_sum([bias_value(ref[ref.shape[0] - BIAS_ROWS:, :]) for ref in refs])
    return weight, bias


def relay_kernel(agg_grad_ref, own_ref, *refs):
    arrived, out_ref = refs[:-1], refs[-1]
    rows = agg_grad_ref.shape[0]
    extra = own_ref.shape[0]
    weight, bias = gradient_sums([own_ref, *arrived], lambda ref: ref.shape[0] - extra)
    out_ref[:rows, :] = agg_grad_ref[...]
    out_ref[rows:-BIAS_ROWS, :] = weight.astype(BF16)
    out_ref[-BIAS_ROWS:, :] = bias_rows(bias)


def relay(agg_grad, own, arrived):
    return pl.pallas_call(
        relay_kernel,
        out_shape=jax.ShapeDtypeStruct(arrived[0].shape, BF16),
        in_specs=[VMEM] * (2 + len(arrived)),
        out_specs=VMEM,
        compiler_params=params(),
        name="relay_message",
    )(agg_grad, own, *arrived)


def totals_kernel(scale, own_ref, *refs):
    arrived, (weight_ref, bias_ref) = refs[:-2], refs[-2:]
    extra = own_ref.shape[0]
    weight, bias = gradient_sums([own_ref, *arrived], lambda ref: ref.shape[0] - extra)
    weight_ref[...] = (weight * scale).astype(BF16)
    bias_ref[...] = bias * scale


def totals(own, arrived, scale):
    extra, width = own.shape
    return pl.pallas_call(
        functools.partial(totals_kernel, scale),
        out_shape=[
            jax.ShapeDtypeStruct((extra - BIAS_ROWS, width), BF16),
            jax.ShapeDtypeStruct((1, width), F32),
        ],
        in_specs=[VMEM] * (1 + len(arrived)),
        out_specs=[VMEM] * 2,
        compiler_params=params(),
        name="gradient_totals",
    )(own, *arrived)


def feature_kernel(own_ref, *refs):
    arrived, out_ref = refs[:-1], refs[-1]
    rows = out_ref.shape[0]
    total = own_ref[...]
    for ref in arrived:
        total = total + ref[:rows, :].astype(F32)
    out_ref[...] = total.astype(BF16)


def feature_sum(own, arrived):
    return pl.pallas_call(
        feature_kernel,
        out_shape=jax.ShapeDtypeStruct(own.shape, BF16),
        in_specs=[VMEM] * (1 + len(arrived)),
        out_specs=VMEM,
        compiler_params=params(),
        name="feature_sum",
    )(own, *arrived)


def assemble_kernel(me_ref, *refs):
    sections, out_ref = refs[:-1], refs[-1]
    chunk = sections[0].shape[0]
    for d, ref in zip([0] + peers(2 * len(sections))[:-1], sections):
        group = jnp.right_shift(jnp.bitwise_xor(me_ref[1], d), 1)
        out_ref[pl.ds(pl.multiple_of(group * chunk, chunk), chunk), :] = ref[...].astype(F32)


def assemble(me, sections):
    chunk, width = sections[0].shape
    return pl.pallas_call(
        assemble_kernel,
        out_shape=jax.ShapeDtypeStruct((chunk * len(sections), width), F32),
        in_specs=[SMEM] + [VMEM] * len(sections),
        out_specs=VMEM,
        compiler_params=params(),
        name="assemble_weight_grad",
    )(me, *sections)


def backward_kernel(count, me_ref, panel_ref, sent_ref, *refs):
    blocks, outs, gathered = refs[:count], refs[count:-1], refs[-1]
    rows = blocks[0].shape[0]
    own_ref, share_ref, messages = outs[0], outs[1], outs[2:]
    weight, bias = gradient_sums([sent_ref, blocks[1]], lambda ref: rows)
    weight, bias_part = weight.astype(BF16), bias_rows(bias)
    row_me, col_me = me_ref[0], me_ref[1]
    for d in range(count):
        source = jnp.bitwise_xor(col_me, d)
        gathered[pl.ds(pl.multiple_of(source * rows, rows), rows), :] = blocks[d][:rows, :]

    def product(d):
        target = jnp.bitwise_xor(row_me, d)
        part = panel_ref[:, pl.ds(pl.multiple_of(target * rows, rows), rows)]
        return lax.dot_general(part, gathered[...], (((0,), (0,)), ((), ())), preferred_element_type=F32)

    for d, message in enumerate(messages, 1):
        message[:rows, :] = product(d).astype(BF16)
        message[rows:-BIAS_ROWS, :] = weight
        message[-BIAS_ROWS:, :] = bias_part
    own_ref[...] = product(0)
    share_ref[:-BIAS_ROWS, :] = weight
    share_ref[-BIAS_ROWS:, :] = bias_part


def backward(me, panel, sent, blocks, row_count):
    rows, width = blocks[0].shape
    size = sent.shape[0]
    out = pl.pallas_call(
        functools.partial(backward_kernel, len(blocks)),
        out_shape=[
            jax.ShapeDtypeStruct((rows, width), F32),
            jax.ShapeDtypeStruct((size - rows, width), BF16),
        ]
        + [jax.ShapeDtypeStruct((size, width), BF16)] * (row_count - 1),
        in_specs=[SMEM, VMEM, VMEM] + [VMEM] * len(blocks),
        out_specs=[VMEM] * (row_count + 1),
        scratch_shapes=[pltpu.VMEM((rows * len(blocks), width), BF16)],
        compiler_params=params(),
        name="backward_terms",
    )(me, panel, sent, *blocks)
    return out[0], out[1], out[2:]


def body(features, weight, bias_vector, out_grad, adj_tiles, tile_pos, tile_count):
    rows_dev, width = features.shape
    tile_size = adj_tiles.shape[-1]
    row_count = lax.axis_size("row")
    col_count = lax.axis_size("col")
    row_tiles = col_count * rows_dev // tile_size
    col_tiles = row_count * rows_dev // tile_size
    me = jnp.stack([lax.axis_index("row"), lax.axis_index("col")]).astype(jnp.int32)

    blocks = [features] + [swapped(features, "row", d) for d in range(1, row_count)]
    panel = build_panel(tile_pos[0, 0], tile_count[0], adj_tiles[0, 0], row_tiles, col_tiles)
    keeps, sends = forward(me, panel, blocks, col_count)
    parts = []
    for d, keep, send in zip(peers(col_count), keeps, sends):
        arrived = swapped(send, "col", 1)
        if d:
            pair = (keep + arrived.astype(F32)).astype(BF16)
            parts.append(swapped(pair, "col", d))
        else:
            parts += [keep, arrived]
    groups = col_count // 2
    order = peers(col_count)[:-1]
    hidden_out, agg_grad, share, *messages = dense(
        me, weight, bias_vector.reshape(1, width), out_grad, parts, groups
    )
    grads = {0: agg_grad}
    for d, message in zip(order, messages):
        grads[d] = swapped(message, "col", d)
    sent = relay(agg_grad, share, [grads[d] for d in tree_order(col_count)])
    grads[1] = swapped(sent, "col", 1)
    for d in order:
        grads[d + 1] = swapped(grads[d][:rows_dev], "col", 1)
    blocks = [grads[d] for d in range(col_count)]
    own, share, messages = backward(me, panel, sent, blocks, row_count)
    arrived = {d: swapped(messages[d - 1], "row", d) for d in range(row_count - 1, 0, -1)}
    arrived = [arrived[d] for d in range(1, row_count)]
    scale = 1.0 / math.sqrt(row_count * col_count * rows_dev)
    section, bias_grad = totals(share, arrived, scale)
    weight_grad = assemble(me, [section] + [swapped(section, "col", d) for d in order])
    feature_grad = feature_sum(own, arrived)
    return (hidden_out, feature_grad, weight_grad, bias_grad.reshape(width))


def solution(mesh):
    in_specs = (
        P(("row", "col"), None),
        P(),
        P(),
        P(("row", "col"), None),
        P("row", "col", None, None, None),
        P("row", "col", None),
        P("row", "col"),
    )
    out_specs = (P(("row", "col"), None), P(("row", "col"), None), P(), P())
    return jax.shard_map(body, mesh=mesh, in_specs=in_specs, out_specs=out_specs, check_vma=False)
```

```python
import functools
import math

import jax
import jax.numpy as jnp
from jax import lax
from jax.experimental import pallas as pl
from jax.experimental.pallas import tpu as pltpu
from jax.sharding import PartitionSpec as P

BF16 = jnp.bfloat16
F32 = jnp.float32
CHUNK = 8
BIAS_ROWS = 16
VMEM = pl.BlockSpec(memory_space=pltpu.VMEM)
ANY = pl.BlockSpec(memory_space=pl.ANY)
SMEM = pl.BlockSpec(memory_space=pltpu.SMEM)


def swapped(block, axis, bit):
    n = lax.axis_size(axis)
    return lax.ppermute(block, axis, [(i, i ^ bit) for i in range(n)])


def params(mib=32):
    return pltpu.CompilerParams(vmem_limit_bytes=mib * 1024 * 1024)


def build_kernel(col_tiles, pos_ref, count_ref, tiles_ref, panel_ref, stage, acc, places, live, sems):
    slots = tiles_ref.shape[0]
    size = tiles_ref.shape[1]
    chunks = slots // CHUNK
    copies = [
        pltpu.make_async_copy(pos_ref, places, sems.at[chunks]),
        pltpu.make_async_copy(count_ref, live, sems.at[chunks + 1]),
    ]
    for chunk in range(chunks):
        part = pl.ds(chunk * CHUNK, CHUNK)
        copies.append(pltpu.make_async_copy(tiles_ref.at[part], stage.at[part], sems.at[chunk]))
    for copy in copies:
        copy.start()
    acc[...] = jnp.zeros_like(acc)
    copies[0].wait()
    copies[1].wait()
    count = live[0, 0]

    def add(slot, carry):
        acc[places[0, slot]] += stage[slot].astype(F32)
        return carry

    for chunk in range(chunks):
        copies[chunk + 2].wait()
        lax.fori_loop(chunk * CHUNK, jnp.minimum(count, (chunk + 1) * CHUNK), add, 0)
    for place in range(acc.shape[0]):
        r, c = place // col_tiles, place % col_tiles
        panel_ref[r * size:(r + 1) * size, c * size:(c + 1) * size] = acc[place].astype(BF16)


def build_panel(positions, count, tiles, row_tiles, col_tiles):
    slots, size = tiles.shape[0], tiles.shape[1]
    places = row_tiles * col_tiles
    return pl.pallas_call(
        functools.partial(build_kernel, col_tiles),
        out_shape=jax.ShapeDtypeStruct((row_tiles * size, col_tiles * size), BF16),
        in_specs=[pl.BlockSpec(memory_space=pltpu.HBM)] * 3,
        out_specs=VMEM,
        scratch_shapes=[
            pltpu.VMEM((slots, size, size), BF16),
            pltpu.VMEM((places, size, size), F32),
            pltpu.SMEM((1, slots), jnp.int32),
            pltpu.SMEM((1, 1), jnp.int32),
            pltpu.SemaphoreType.DMA((slots // CHUNK + 2,)),
        ],
        compiler_params=params(max(52, (slots * 2 + places * 6) * size * size // 2**20 + 4)),
        cost_estimate=pl.CostEstimate(
            flops=slots * size * size, bytes_accessed=2 * slots * size * size, transcendentals=0
        ),
        name="build_panel",
    )(positions, count, tiles)


def peers(count):
    return sorted(range(2, count, 2), key=lambda d: (abs(d - count // 2 - 0.5), d)) + [0]


def forward_kernel(count, flip, panel_ref, *refs):
    blocks, outs, gathered = refs[:count], refs[count:-1], refs[-1]
    rows = blocks[0].shape[0]
    row_me, col_me = lax.axis_index("row"), lax.axis_index("col")
    for d in range(count):
        source = jnp.bitwise_xor(row_me, d)
        gathered[pl.ds(pl.multiple_of(source * rows, rows), rows), :] = blocks[d][...]
    for d, out in zip(peers(2 * len(outs)), outs):
        target = jnp.bitwise_xor(col_me, d + flip)
        part = panel_ref[pl.ds(pl.multiple_of(target * rows, rows), rows), :]
        out[...] = jnp.dot(part, gathered[...], preferred_element_type=F32).astype(out.dtype)


def forward(panel, blocks, half, flip, dtype):
    rows, width = blocks[0].shape
    return pl.pallas_call(
        functools.partial(forward_kernel, len(blocks), flip),
        out_shape=[jax.ShapeDtypeStruct((rows, width), dtype)] * half,
        in_specs=[VMEM] * (1 + len(blocks)),
        out_specs=[VMEM] * half,
        scratch_shapes=[pltpu.VMEM((rows * len(blocks), width), BF16)],
        compiler_params=params(),
        name="forward_partial",
    )(panel, *blocks)


def split_bias(value):
    high = value.astype(BF16)
    low = (value - high.astype(F32)).astype(BF16)
    return high, low


def bias_rows(value):
    high, low = split_bias(value)
    row = lax.broadcasted_iota(jnp.int32, (BIAS_ROWS, value.shape[1]), 0)
    high, low = high.astype(F32), low.astype(F32)
    return jnp.where(row == 0, high, jnp.where(row == 1, low, 0.0)).astype(BF16)


def bias_value(rows):
    return jnp.sum(rows.astype(F32), axis=0, keepdims=True)


def split_rows(bit, whole, bias_part, keep_ref, send_ref):
    half = whole.shape[0] // 2
    mine = jnp.where(jnp.bitwise_and(lax.axis_index("row"), bit) != 0, half, 0)
    keep_ref[:half, :] = whole[pl.ds(pl.multiple_of(mine, half), half), :]
    send_ref[:half, :] = whole[pl.ds(pl.multiple_of(half - mine, half), half), :]
    keep_ref[half:, :] = bias_part
    send_ref[half:, :] = bias_part


def dense_kernel(count, weight_ref, bias_ref, grad_ref, *refs):
    parts, outs = refs[:count], refs[count:]
    hidden_ref, agg_grad_ref, keep_ref, send_ref, weights = outs
    total = parts[0][...].astype(F32)
    for part in parts[1:]:
        total = total + part[...].astype(F32)
    aggregated = total.astype(BF16)
    weight = weight_ref[...]
    pre = jnp.dot(aggregated, weight, preferred_element_type=F32) + bias_ref[...]
    gate = jax.nn.sigmoid(pre)
    hidden_ref[...] = (pre * gate).astype(BF16)
    pre_grad = (grad_ref[...].astype(F32) * (gate * (1.0 + pre * (1.0 - gate)))).astype(BF16)
    agg_grad = lax.dot_general(
        pre_grad, weight, (((1,), (1,)), ((), ())), preferred_element_type=F32
    ).astype(BF16)
    agg_grad_ref[...] = agg_grad
    weights[...] = lax.dot_general(
        aggregated, pre_grad, (((0,), (0,)), ((), ())), preferred_element_type=F32
    ).astype(BF16)
    bias_part = bias_rows(jnp.sum(pre_grad.astype(F32), axis=0, keepdims=True))

    split_rows(1, weights, bias_part, keep_ref, send_ref)


def dense(weight, bias_vector, out_grad, parts):
    width = out_grad.shape[1]
    extra = width // 2 + BIAS_ROWS
    return pl.pallas_call(
        functools.partial(dense_kernel, len(parts)),
        out_shape=[jax.ShapeDtypeStruct(out_grad.shape, BF16)] * 2
        + [jax.ShapeDtypeStruct((extra, width), BF16)] * 2,
        in_specs=[VMEM] * (3 + len(parts)),
        out_specs=[VMEM] * 4,
        scratch_shapes=[pltpu.VMEM(weight.shape, BF16)],
        compiler_params=params(),
        name="dense_stage",
    )(weight, bias_vector, out_grad, *parts)


def tree_sum(values):
    while len(values) > 1:
        values = [values[k] + values[k + 1] for k in range(0, len(values), 2)]
    return values[0]


def gradient_sums(refs, start):
    weight = tree_sum([ref[start(ref):ref.shape[0] - BIAS_ROWS, :].astype(F32) for ref in refs])
    bias = tree_sum([bias_value(ref[ref.shape[0] - BIAS_ROWS:, :]) for ref in refs])
    return weight, bias


def relay_kernel(agg_grad_ref, left_ref, right_ref, *refs):
    shares, out_ref = [left_ref, right_ref], refs[-1]
    rows = agg_grad_ref.shape[0]
    weight, bias = gradient_sums(shares, lambda ref: 0)
    out_ref[:rows, :] = agg_grad_ref[...]
    out_ref[rows:-BIAS_ROWS, :] = weight.astype(BF16)
    out_ref[-BIAS_ROWS:, :] = bias_rows(bias)


def relay(agg_grad, shares, after):
    size = agg_grad.shape[0] + shares[0].shape[0]
    return pl.pallas_call(
        relay_kernel,
        out_shape=jax.ShapeDtypeStruct((size, agg_grad.shape[1]), BF16),
        in_specs=[VMEM] * 3 + [ANY] * len(after),
        out_specs=VMEM,
        compiler_params=params(),
        name="relay_message",
    )(agg_grad, *shares, *after)


def split_kernel(bit, left_ref, right_ref, keep_ref, send_ref, whole):
    weight, bias = gradient_sums([left_ref, right_ref], lambda ref: 0)
    whole[...] = weight.astype(BF16)
    split_rows(bit, whole, bias_rows(bias), keep_ref, send_ref)


def split_sum(bit, left, right):
    rows, width = left.shape[0] - BIAS_ROWS, left.shape[1]
    return pl.pallas_call(
        functools.partial(split_kernel, bit),
        out_shape=[jax.ShapeDtypeStruct((rows // 2 + BIAS_ROWS, width), BF16)] * 2,
        in_specs=[VMEM, VMEM],
        out_specs=[VMEM, VMEM],
        scratch_shapes=[pltpu.VMEM((rows, width), BF16)],
        compiler_params=params(),
        name="split_sum",
    )(left, right)


def pair_kernel(extra, left_ref, right_ref, out_ref):
    weight, bias = gradient_sums([left_ref, right_ref], lambda ref: ref.shape[0] - extra)
    out_ref[:-BIAS_ROWS, :] = weight.astype(BF16)
    out_ref[-BIAS_ROWS:, :] = bias_rows(bias)


def pair_sum(extra, left, right):
    return pl.pallas_call(
        functools.partial(pair_kernel, extra),
        out_shape=jax.ShapeDtypeStruct((extra, left.shape[1]), BF16),
        in_specs=[VMEM, VMEM],
        out_specs=VMEM,
        compiler_params=params(),
        name="pair_sum",
    )(left, right)


def totals_kernel(scale, *refs):
    shares, (weight_ref, bias_ref) = refs[:-2], refs[-2:]
    weight, bias = gradient_sums(shares, lambda ref: 0)
    weight_ref[...] = (weight * scale).astype(BF16)
    bias_ref[...] = bias * scale


def totals(shares, scale):
    extra, width = shares[0].shape
    return pl.pallas_call(
        functools.partial(totals_kernel, scale),
        out_shape=[
            jax.ShapeDtypeStruct((extra - BIAS_ROWS, width), BF16),
            jax.ShapeDtypeStruct((1, width), F32),
        ],
        in_specs=[VMEM] * len(shares),
        out_specs=[VMEM] * 2,
        compiler_params=params(),
        name="gradient_totals",
    )(*shares)


def halve_kernel(keep_ref, arrived_ref, rest_ref, send_ref):
    half = rest_ref.shape[0]
    rest_ref[...] = keep_ref[:half, :] + arrived_ref[:half, :].astype(F32)
    send_ref[...] = (keep_ref[half:, :] + arrived_ref[half:, :].astype(F32)).astype(BF16)


def halve(keep, arrived):
    shape = (keep.shape[0] // 2, keep.shape[1])
    return pl.pallas_call(
        halve_kernel,
        out_shape=[jax.ShapeDtypeStruct(shape, F32), jax.ShapeDtypeStruct(shape, BF16)],
        in_specs=[VMEM, VMEM],
        out_specs=[VMEM, VMEM],
        compiler_params=params(),
        name="halve_terms",
    )(keep, arrived)


def feature_kernel(own_ref, arrived_ref, out_ref, token_ref):
    token_ref[...] = jnp.zeros_like(token_ref)
    out_ref[...] = (own_ref[...] + arrived_ref[...].astype(F32)).astype(BF16)


def feature_sum(own, arrived):
    return pl.pallas_call(
        feature_kernel,
        out_shape=[jax.ShapeDtypeStruct(own.shape, BF16), jax.ShapeDtypeStruct((8, 128), F32)],
        in_specs=[VMEM, VMEM],
        out_specs=[VMEM, VMEM],
        compiler_params=params(),
        name="feature_sum",
    )(own, arrived)


def assemble_kernel(after_ref, *refs):
    sections, out_ref = refs[:-1], refs[-1]
    chunk, count = sections[0].shape[0], len(sections)
    for d, ref in enumerate(sections):
        device, start, bit = jnp.bitwise_xor(lax.axis_index("row"), d), 0, 1
        while bit < count:
            start += jnp.where(jnp.bitwise_and(device, bit) != 0, chunk * count // (2 * bit), 0)
            bit *= 2
        out_ref[pl.ds(pl.multiple_of(start, chunk), chunk), :] = ref[...].astype(F32)


def assemble(after, sections):
    chunk, width = sections[0].shape
    return pl.pallas_call(
        assemble_kernel,
        out_shape=jax.ShapeDtypeStruct((chunk * len(sections), width), F32),
        in_specs=[ANY] + [VMEM] * len(sections),
        out_specs=VMEM,
        compiler_params=params(),
        name="assemble_weight_grad",
    )(after, *sections)


def backward_kernel(count, flip, panel_ref, *refs):
    blocks, (out_ref, gathered) = refs[:count], (refs[-2], refs[-1])
    rows = gathered.shape[0] // count
    row_me, col_me = lax.axis_index("row"), lax.axis_index("col")
    for d in range(count):
        source = jnp.bitwise_xor(col_me, d)
        gathered[pl.ds(pl.multiple_of(source * rows, rows), rows), :] = blocks[d][:rows, :]
    for k in range(out_ref.shape[0] // rows):
        target = jnp.bitwise_xor(row_me, 2 * k + flip)
        part = panel_ref[:, pl.ds(pl.multiple_of(target * rows, rows), rows)]
        value = lax.dot_general(part, gathered[...], (((0,), (0,)), ((), ())), preferred_element_type=F32)
        out_ref[k * rows:(k + 1) * rows, :] = value.astype(out_ref.dtype)


def backward(panel, blocks, after, half, flip, dtype):
    rows, width = blocks[0].shape
    return pl.pallas_call(
        functools.partial(backward_kernel, len(blocks), flip),
        out_shape=jax.ShapeDtypeStruct((rows * half, width), dtype),
        in_specs=[VMEM] * (1 + len(blocks)) + [ANY] * len(after),
        out_specs=VMEM,
        scratch_shapes=[pltpu.VMEM((rows * len(blocks), width), BF16)],
        compiler_params=params(),
        name="backward_terms",
    )(panel, *blocks, *after)


def body(features, weight, bias_vector, out_grad, adj_tiles, tile_pos, tile_count):
    rows_dev, width = features.shape
    tile_size = adj_tiles.shape[-1]
    row_count = lax.axis_size("row")
    col_count = lax.axis_size("col")
    row_tiles = col_count * rows_dev // tile_size
    col_tiles = row_count * rows_dev // tile_size

    blocks = [features] + [swapped(features, "row", d) for d in range(1, row_count)]
    panel = build_panel(tile_pos[0], tile_count, adj_tiles[0, 0], row_tiles, col_tiles)
    sends = forward(panel, blocks, col_count // 2, 1, BF16)
    keeps = forward(panel, blocks, col_count // 2, 0, F32)
    parts = []
    for d, keep, send in zip(peers(col_count), keeps, sends):
        arrived = swapped(send, "col", 1)
        if d:
            pair = (keep + arrived.astype(F32)).astype(BF16)
            parts.append(swapped(pair, "col", d))
        else:
            parts += [keep, arrived]
    order = peers(col_count)[:-1]
    hidden_out, agg_grad, share, send = dense(
        weight, bias_vector.reshape(1, width), out_grad, parts
    )
    arrived = swapped(send, "row", 1)
    grads = {0: agg_grad}
    for d in order:
        grads[d] = swapped(agg_grad, "col", d)
    bit = 2
    while bit < row_count:
        share, send = split_sum(bit, share, arrived)
        arrived = swapped(send, "row", bit)
        bit *= 2
    extra = share.shape[0]
    sent = relay(agg_grad, [share, arrived], [grads[d] for d in order[:-1]])
    grads[1] = swapped(sent, "col", 1)
    for d in order:
        grads[d + 1] = swapped(grads[d], "col", 1)
    blocks = [grads[d] for d in range(col_count)]
    share = pair_sum(extra, sent, grads[1])
    shares = {d: swapped(share, "col", d) for d in order}
    shares = [share] + [shares[d] for d in range(2, col_count, 2)]

    send = backward(panel, blocks, shares[1:], row_count // 2, 1, BF16)
    keep = backward(panel, blocks, [], row_count // 2, 0, F32)
    terms = swapped(send, "row", 1)
    bit = row_count // 2
    while bit > 1:
        keep, send = halve(keep, terms)
        terms = swapped(send, "row", bit)
        bit //= 2
    feature_grad, token = feature_sum(keep, terms)
    scale = 1.0 / math.sqrt(row_count * col_count * rows_dev)
    section, bias_grad = totals(shares, scale)
    sections = [section] + [swapped(section, "row", d) for d in range(1, row_count)]
    weight_grad = assemble(token, sections)
    return (hidden_out, feature_grad, weight_grad, bias_grad.reshape(width))


def solution(mesh):
    in_specs = (
        P(("row", "col"), None),
        P(),
        P(),
        P(("row", "col"), None),
        P("row", "col", None, None, None),
        P("row", "col", None),
        P("row", "col"),
    )
    out_specs = (P(("row", "col"), None), P(("row", "col"), None), P(), P())
    return jax.shard_map(body, mesh=mesh, in_specs=in_specs, out_specs=out_specs, check_vma=False)
```

```python
import functools
import math

import jax
import jax.numpy as jnp
from jax import lax
from jax.experimental import pallas as pl
from jax.experimental.pallas import tpu as pltpu
from jax.sharding import PartitionSpec as P

BF16 = jnp.bfloat16
F32 = jnp.float32
CHUNK = 8
BIAS_ROWS = 16
VMEM = pl.BlockSpec(memory_space=pltpu.VMEM)
ANY = pl.BlockSpec(memory_space=pl.ANY)
SMEM = pl.BlockSpec(memory_space=pltpu.SMEM)


def swapped(block, axis, bit):
    n = lax.axis_size(axis)
    return lax.ppermute(block, axis, [(i, i ^ bit) for i in range(n)])


def params(mib=32):
    return pltpu.CompilerParams(vmem_limit_bytes=mib * 1024 * 1024)


def build_kernel(col_tiles, pos_ref, count_ref, tiles_ref, panel_ref, stage, acc, places, live, sems):
    slots = tiles_ref.shape[0]
    size = tiles_ref.shape[1]
    chunks = slots // CHUNK
    copies = [
        pltpu.make_async_copy(pos_ref, places, sems.at[chunks]),
        pltpu.make_async_copy(count_ref, live, sems.at[chunks + 1]),
    ]
    for chunk in range(chunks):
        part = pl.ds(chunk * CHUNK, CHUNK)
        copies.append(pltpu.make_async_copy(tiles_ref.at[part], stage.at[part], sems.at[chunk]))
    for copy in copies:
        copy.start()
    acc[...] = jnp.zeros_like(acc)
    copies[0].wait()
    copies[1].wait()
    count = live[0, 0]

    def add(slot, carry):
        acc[places[0, slot]] += stage[slot].astype(F32)
        return carry

    for chunk in range(chunks):
        copies[chunk + 2].wait()
        lax.fori_loop(chunk * CHUNK, jnp.minimum(count, (chunk + 1) * CHUNK), add, 0)
    for place in range(acc.shape[0]):
        r, c = place // col_tiles, place % col_tiles
        panel_ref[r * size:(r + 1) * size, c * size:(c + 1) * size] = acc[place].astype(BF16)


def build_panel(positions, count, tiles, row_tiles, col_tiles):
    slots, size = tiles.shape[0], tiles.shape[1]
    places = row_tiles * col_tiles
    return pl.pallas_call(
        functools.partial(build_kernel, col_tiles),
        out_shape=jax.ShapeDtypeStruct((row_tiles * size, col_tiles * size), BF16),
        in_specs=[pl.BlockSpec(memory_space=pltpu.HBM)] * 3,
        out_specs=VMEM,
        scratch_shapes=[
            pltpu.VMEM((slots, size, size), BF16),
            pltpu.VMEM((places, size, size), F32),
            pltpu.SMEM((1, slots), jnp.int32),
            pltpu.SMEM((1, 1), jnp.int32),
            pltpu.SemaphoreType.DMA((slots // CHUNK + 2,)),
        ],
        compiler_params=params(max(52, (slots * 2 + places * 6) * size * size // 2**20 + 4)),
        cost_estimate=pl.CostEstimate(
            flops=slots * size * size, bytes_accessed=2 * slots * size * size, transcendentals=0
        ),
        name="build_panel",
    )(positions, count, tiles)


def peers(count):
    return sorted(range(2, count, 2), key=lambda d: (abs(d - count // 2 - 0.5), d)) + [0]


def forward_kernel(count, flip, panel_ref, *refs):
    blocks, outs, gathered = refs[:count], refs[count:-1], refs[-1]
    rows = blocks[0].shape[0]
    row_me, col_me = lax.axis_index("row"), lax.axis_index("col")
    for d in range(count):
        source = jnp.bitwise_xor(row_me, d)
        gathered[pl.ds(pl.multiple_of(source * rows, rows), rows), :] = blocks[d][...]
    for d, out in zip(peers(2 * len(outs)), outs):
        target = jnp.bitwise_xor(col_me, d + flip)
        part = panel_ref[pl.ds(pl.multiple_of(target * rows, rows), rows), :]
        out[...] = jnp.dot(part, gathered[...], preferred_element_type=F32).astype(out.dtype)


def forward(panel, blocks, half, flip, dtype):
    rows, width = blocks[0].shape
    return pl.pallas_call(
        functools.partial(forward_kernel, len(blocks), flip),
        out_shape=[jax.ShapeDtypeStruct((rows, width), dtype)] * half,
        in_specs=[VMEM] * (1 + len(blocks)),
        out_specs=[VMEM] * half,
        scratch_shapes=[pltpu.VMEM((rows * len(blocks), width), BF16)],
        compiler_params=params(),
        name="forward_partial",
    )(panel, *blocks)


def split_bias(value):
    high = value.astype(BF16)
    low = (value - high.astype(F32)).astype(BF16)
    return high, low


def bias_rows(value):
    high, low = split_bias(value)
    row = lax.broadcasted_iota(jnp.int32, (BIAS_ROWS, value.shape[1]), 0)
    high, low = high.astype(F32), low.astype(F32)
    return jnp.where(row == 0, high, jnp.where(row == 1, low, 0.0)).astype(BF16)


def bias_value(rows):
    return jnp.sum(rows.astype(F32), axis=0, keepdims=True)


def split_rows(bit, whole, bias_part, keep_ref, send_ref):
    half = whole.shape[0] // 2
    mine = jnp.where(jnp.bitwise_and(lax.axis_index("row"), bit) != 0, half, 0)
    keep_ref[:half, :] = whole[pl.ds(pl.multiple_of(mine, half), half), :]
    send_ref[:half, :] = whole[pl.ds(pl.multiple_of(half - mine, half), half), :]
    keep_ref[half:, :] = bias_part
    send_ref[half:, :] = bias_part


def dense_kernel(count, weight_ref, bias_ref, grad_ref, *refs):
    parts, outs = refs[:count], refs[count:]
    hidden_ref, agg_grad_ref, keep_ref, send_ref, weights = outs
    total = parts[0][...].astype(F32)
    for part in parts[1:]:
        total = total + part[...].astype(F32)
    aggregated = total.astype(BF16)
    weight = weight_ref[...]
    pre = jnp.dot(aggregated, weight, preferred_element_type=F32) + bias_ref[...]
    gate = jax.nn.sigmoid(pre)
    hidden_ref[...] = (pre * gate).astype(BF16)
    pre_grad = (grad_ref[...].astype(F32) * (gate * (1.0 + pre * (1.0 - gate)))).astype(BF16)
    agg_grad = lax.dot_general(
        pre_grad, weight, (((1,), (1,)), ((), ())), preferred_element_type=F32
    ).astype(BF16)
    agg_grad_ref[...] = agg_grad
    weights[...] = lax.dot_general(
        aggregated, pre_grad, (((0,), (0,)), ((), ())), preferred_element_type=F32
    ).astype(BF16)
    bias_part = bias_rows(jnp.sum(pre_grad.astype(F32), axis=0, keepdims=True))

    split_rows(1, weights, bias_part, keep_ref, send_ref)


def dense(weight, bias_vector, out_grad, parts):
    width = out_grad.shape[1]
    extra = width // 2 + BIAS_ROWS
    return pl.pallas_call(
        functools.partial(dense_kernel, len(parts)),
        out_shape=[jax.ShapeDtypeStruct(out_grad.shape, BF16)] * 2
        + [jax.ShapeDtypeStruct((extra, width), BF16)] * 2,
        in_specs=[VMEM] * (3 + len(parts)),
        out_specs=[VMEM] * 4,
        scratch_shapes=[pltpu.VMEM(weight.shape, BF16)],
        compiler_params=params(),
        name="dense_stage",
    )(weight, bias_vector, out_grad, *parts)


def tree_sum(values):
    while len(values) > 1:
        values = [values[k] + values[k + 1] for k in range(0, len(values), 2)]
    return values[0]


def gradient_sums(refs, start):
    weight = tree_sum([ref[start(ref):ref.shape[0] - BIAS_ROWS, :].astype(F32) for ref in refs])
    bias = tree_sum([bias_value(ref[ref.shape[0] - BIAS_ROWS:, :]) for ref in refs])
    return weight, bias


def split_kernel(bit, left_ref, right_ref, keep_ref, send_ref, whole):
    weight, bias = gradient_sums([left_ref, right_ref], lambda ref: 0)
    whole[...] = weight.astype(BF16)
    split_rows(bit, whole, bias_rows(bias), keep_ref, send_ref)


def split_sum(bit, left, right):
    rows, width = left.shape[0] - BIAS_ROWS, left.shape[1]
    return pl.pallas_call(
        functools.partial(split_kernel, bit),
        out_shape=[jax.ShapeDtypeStruct((rows // 2 + BIAS_ROWS, width), BF16)] * 2,
        in_specs=[VMEM, VMEM],
        out_specs=[VMEM, VMEM],
        scratch_shapes=[pltpu.VMEM((rows, width), BF16)],
        compiler_params=params(),
        name="split_sum",
    )(left, right)


def sum_kernel(count, *refs):
    weight, bias = gradient_sums(refs[:count], lambda ref: 0)
    out_ref = refs[-1]
    out_ref[:-BIAS_ROWS, :] = weight.astype(BF16)
    out_ref[-BIAS_ROWS:, :] = bias_rows(bias)


def sum_shares(shares, after):
    return pl.pallas_call(
        functools.partial(sum_kernel, len(shares)),
        out_shape=jax.ShapeDtypeStruct(shares[0].shape, BF16),
        in_specs=[VMEM] * len(shares) + [ANY] * len(after),
        out_specs=VMEM,
        compiler_params=params(),
        name="sum_shares",
    )(*shares, *after)


def halve_kernel(keep_ref, sent_ref, arrived_ref, rest_ref, send_ref):
    rows, half = keep_ref.shape[0], rest_ref.shape[0]
    held = sent_ref.shape[0] - rows
    rest_ref[...] = keep_ref[:half, :] + arrived_ref[:half, :].astype(F32)
    send_ref[:half, :] = (keep_ref[half:, :] + arrived_ref[half:rows, :].astype(F32)).astype(BF16)
    send_ref[half:half + held, :] = sent_ref[rows:, :]
    send_ref[half + held:, :] = arrived_ref[rows:, :]


def halve(keep, sent, arrived):
    rows, width = keep.shape
    size = rows // 2 + 2 * (sent.shape[0] - rows)
    return pl.pallas_call(
        halve_kernel,
        out_shape=[
            jax.ShapeDtypeStruct((rows // 2, width), F32),
            jax.ShapeDtypeStruct((size, width), BF16),
        ],
        in_specs=[VMEM] * 3,
        out_specs=[VMEM, VMEM],
        compiler_params=params(),
        name="halve_terms",
    )(keep, sent, arrived)


def final_kernel(owners, keep_ref, sent_ref, arrived_ref, feature_ref, weight_ref):
    rows = keep_ref.shape[0]
    feature_ref[...] = (keep_ref[...] + arrived_ref[:rows, :].astype(F32)).astype(BF16)
    count = len(owners)
    chunk = weight_ref.shape[0] // count
    for k, d in enumerate(owners):
        device, start, bit = jnp.bitwise_xor(lax.axis_index("row"), d), 0, 1
        while bit < count:
            start += jnp.where(jnp.bitwise_and(device, bit) != 0, chunk * count // (2 * bit), 0)
            bit *= 2
        source, place = (sent_ref, k) if k < count // 2 else (arrived_ref, k - count // 2)
        value = source[rows + place * chunk:rows + (place + 1) * chunk, :].astype(F32)
        weight_ref[pl.ds(pl.multiple_of(start, chunk), chunk), :] = value


def final(owners, keep, sent, arrived):
    rows, width = keep.shape
    return pl.pallas_call(
        functools.partial(final_kernel, owners),
        out_shape=[
            jax.ShapeDtypeStruct((rows, width), BF16),
            jax.ShapeDtypeStruct((2 * (sent.shape[0] - rows), width), F32),
        ],
        in_specs=[VMEM] * 3,
        out_specs=[VMEM, VMEM],
        compiler_params=params(),
        name="final_sums",
    )(keep, sent, arrived)


def gather_terms(blocks, gathered):
    rows = blocks[0].shape[0]
    for d, block in enumerate(blocks):
        source = jnp.bitwise_xor(lax.axis_index("col"), d)
        gathered[pl.ds(pl.multiple_of(source * rows, rows), rows), :] = block[...]


def term(panel_ref, gathered, rows, d):
    target = jnp.bitwise_xor(lax.axis_index("row"), d)
    part = panel_ref[:, pl.ds(pl.multiple_of(target * rows, rows), rows)]
    return lax.dot_general(part, gathered[...], (((0,), (0,)), ((), ())), preferred_element_type=F32)


def send_kernel(count, scale, panel_ref, left_ref, right_ref, *refs):
    blocks, (send_ref, gathered) = refs[:count], refs[count:]
    rows = blocks[0].shape[0]
    gather_terms(blocks, gathered)
    weight, _ = gradient_sums([left_ref, right_ref], lambda ref: 0)
    half = send_ref.shape[0] - weight.shape[0]
    send_ref[half:, :] = (weight * scale).astype(BF16)
    for k in range(half // rows):
        send_ref[k * rows:(k + 1) * rows, :] = term(panel_ref, gathered, rows, 2 * k + 1).astype(BF16)


def backward_send(panel, blocks, left, right, half, scale):
    rows, width = blocks[0].shape
    return pl.pallas_call(
        functools.partial(send_kernel, len(blocks), scale),
        out_shape=jax.ShapeDtypeStruct((rows * half + left.shape[0] - BIAS_ROWS, width), BF16),
        in_specs=[VMEM] * (3 + len(blocks)),
        out_specs=VMEM,
        scratch_shapes=[pltpu.VMEM((rows * len(blocks), width), BF16)],
        compiler_params=params(),
        name="backward_send",
    )(panel, left, right, *blocks)


def keep_kernel(count, scale, panel_ref, left_ref, right_ref, *refs):
    blocks, (keep_ref, bias_ref, gathered) = refs[:count], refs[count:]
    rows = blocks[0].shape[0]
    gather_terms(blocks, gathered)
    bias_ref[...] = gradient_sums([left_ref, right_ref], lambda ref: 0)[1] * scale
    for k in range(keep_ref.shape[0] // rows):
        keep_ref[k * rows:(k + 1) * rows, :] = term(panel_ref, gathered, rows, 2 * k)


def backward_keep(panel, blocks, left, right, half, scale):
    rows, width = blocks[0].shape
    return pl.pallas_call(
        functools.partial(keep_kernel, len(blocks), scale),
        out_shape=[
            jax.ShapeDtypeStruct((rows * half, width), F32),
            jax.ShapeDtypeStruct((1, width), F32),
        ],
        in_specs=[VMEM] * (3 + len(blocks)),
        out_specs=[VMEM, VMEM],
        scratch_shapes=[pltpu.VMEM((rows * len(blocks), width), BF16)],
        compiler_params=params(),
        name="backward_keep",
    )(panel, left, right, *blocks)


def body(features, weight, bias_vector, out_grad, adj_tiles, tile_pos, tile_count):
    rows_dev, width = features.shape
    tile_size = adj_tiles.shape[-1]
    row_count = lax.axis_size("row")
    col_count = lax.axis_size("col")
    row_tiles = col_count * rows_dev // tile_size
    col_tiles = row_count * rows_dev // tile_size

    blocks = [features] + [swapped(features, "row", d) for d in range(1, row_count)]
    panel = build_panel(pltpu.with_memory_space_constraint(tile_pos[0], pltpu.HBM), tile_count, adj_tiles[0, 0], row_tiles, col_tiles)
    sends = forward(panel, blocks, col_count // 2, 1, BF16)
    keeps = forward(panel, blocks, col_count // 2, 0, F32)
    parts = []
    for d, keep, send in zip(peers(col_count), keeps, sends):
        arrived = swapped(send, "col", 1)
        if d:
            pair = (keep + arrived.astype(F32)).astype(BF16)
            parts.append(swapped(pair, "col", d))
        else:
            parts += [keep, arrived]
    order = peers(col_count)[:-1]
    hidden_out, agg_grad, share, send = dense(
        weight, bias_vector.reshape(1, width), out_grad, parts
    )
    arrived = swapped(send, "row", 1)
    grads = {0: agg_grad}
    for d in order:
        grads[d] = swapped(agg_grad, "col", d)
    bit = 2
    while bit < row_count:
        share, send = split_sum(bit, share, arrived)
        arrived = swapped(send, "row", bit)
        bit *= 2
    grads[1] = swapped(agg_grad, "col", 1)
    for d in order:
        grads[d + 1] = swapped(grads[d], "col", 1)
    blocks = [grads[d] for d in range(col_count)]
    share = sum_shares([share, arrived], [grads[d] for d in order[:-1]])
    shares = {d: swapped(share, "col", d) for d in order}
    shares = [share] + [shares[d] for d in range(2, col_count, 2)]
    share = sum_shares(shares, [grads[d + 1] for d in order[:1]])
    arrived = swapped(share, "col", 1)

    scale = 1.0 / math.sqrt(row_count * col_count * rows_dev)
    pair = (share, arrived, row_count // 2, scale)
    sent = backward_send(panel, blocks, *pair)
    keep, bias_grad = backward_keep(panel, blocks, *pair)
    terms = swapped(sent, "row", 1)
    owners, bit = [0, 1], row_count // 2
    while bit > 1:
        keep, sent = halve(keep, sent, terms)
        terms = swapped(sent, "row", bit)
        owners = owners + [d ^ bit for d in owners]
        bit //= 2
    feature_grad, weight_grad = final(owners, keep, sent, terms)
    return (hidden_out, feature_grad, weight_grad, bias_grad.reshape(width))


def solution(mesh):
    in_specs = (
        P(("row", "col"), None),
        P(),
        P(),
        P(("row", "col"), None),
        P("row", "col", None, None, None),
        P("row", "col", None),
        P("row", "col"),
    )
    out_specs = (P(("row", "col"), None), P(("row", "col"), None), P(), P())
    return jax.shard_map(body, mesh=mesh, in_specs=in_specs, out_specs=out_specs, check_vma=False)
```

```python
import functools
import math

import jax
import jax.numpy as jnp
from jax import lax
from jax.experimental import pallas as pl
from jax.experimental.pallas import tpu as pltpu
from jax.sharding import PartitionSpec as P

BF16 = jnp.bfloat16
F32 = jnp.float32
CHUNK = 8
BIAS_ROWS = 16
VMEM = pl.BlockSpec(memory_space=pltpu.VMEM)
ANY = pl.BlockSpec(memory_space=pl.ANY)
SMEM = pl.BlockSpec(memory_space=pltpu.SMEM)


def swapped(block, axis, bit):
    n = lax.axis_size(axis)
    return lax.ppermute(block, axis, [(i, i ^ bit) for i in range(n)])


def params(mib=32):
    return pltpu.CompilerParams(vmem_limit_bytes=mib * 1024 * 1024)


def build_kernel(col_tiles, pos_ref, count_ref, tiles_ref, panel_ref, stage, acc, places, live, sems):
    slots = tiles_ref.shape[0]
    size = tiles_ref.shape[1]
    chunks = slots // CHUNK
    copies = [
        pltpu.make_async_copy(pos_ref, places, sems.at[chunks]),
        pltpu.make_async_copy(count_ref, live, sems.at[chunks + 1]),
    ]
    for chunk in range(chunks):
        part = pl.ds(chunk * CHUNK, CHUNK)
        copies.append(pltpu.make_async_copy(tiles_ref.at[part], stage.at[part], sems.at[chunk]))
    for copy in copies:
        copy.start()
    acc[...] = jnp.zeros_like(acc)
    copies[0].wait()
    copies[1].wait()
    count = live[0, 0]

    def add(slot, carry):
        acc[places[0, slot]] += stage[slot].astype(F32)
        return carry

    for chunk in range(chunks):
        copies[chunk + 2].wait()
        lax.fori_loop(chunk * CHUNK, jnp.minimum(count, (chunk + 1) * CHUNK), add, 0)
    for place in range(acc.shape[0]):
        r, c = place // col_tiles, place % col_tiles
        panel_ref[r * size:(r + 1) * size, c * size:(c + 1) * size] = acc[place].astype(BF16)


def build_panel(positions, count, tiles, row_tiles, col_tiles):
    slots, size = tiles.shape[0], tiles.shape[1]
    places = row_tiles * col_tiles
    return pl.pallas_call(
        functools.partial(build_kernel, col_tiles),
        out_shape=jax.ShapeDtypeStruct((row_tiles * size, col_tiles * size), BF16),
        in_specs=[pl.BlockSpec(memory_space=pltpu.HBM)] * 3,
        out_specs=VMEM,
        scratch_shapes=[
            pltpu.VMEM((slots, size, size), BF16),
            pltpu.VMEM((places, size, size), F32),
            pltpu.SMEM((1, slots), jnp.int32),
            pltpu.SMEM((1, 1), jnp.int32),
            pltpu.SemaphoreType.DMA((slots // CHUNK + 2,)),
        ],
        compiler_params=params(max(52, (slots * 2 + places * 6) * size * size // 2**20 + 4)),
        cost_estimate=pl.CostEstimate(
            flops=slots * size * size, bytes_accessed=2 * slots * size * size, transcendentals=0
        ),
        name="build_panel",
    )(positions, count, tiles)


def peers(count):
    return sorted(range(2, count, 2), key=lambda d: (abs(d - count // 2 - 0.5), d)) + [0]


def copy_kernel(block_ref, after_ref, out_ref):
    out_ref[...] = block_ref[...]


def copied(block, after):
    return pl.pallas_call(
        copy_kernel,
        out_shape=jax.ShapeDtypeStruct(block.shape, block.dtype),
        in_specs=[VMEM, ANY],
        out_specs=VMEM,
        compiler_params=params(),
        name="copy_block",
    )(block, after)


def forward_kernel(count, flip, panel_ref, *refs):
    blocks, outs, gathered = refs[:count], refs[count:-1], refs[-1]
    rows = blocks[0].shape[0]
    row_me, col_me = lax.axis_index("row"), lax.axis_index("col")
    for d in range(count):
        source = jnp.bitwise_xor(row_me, d)
        gathered[pl.ds(pl.multiple_of(source * rows, rows), rows), :] = blocks[d][...]
    for d, out in zip(peers(2 * len(outs)), outs):
        target = jnp.bitwise_xor(col_me, d + flip)
        part = panel_ref[pl.ds(pl.multiple_of(target * rows, rows), rows), :]
        out[...] = jnp.dot(part, gathered[...], preferred_element_type=F32).astype(out.dtype)


def forward(panel, blocks, half, flip, dtype):
    rows, width = blocks[0].shape
    return pl.pallas_call(
        functools.partial(forward_kernel, len(blocks), flip),
        out_shape=[jax.ShapeDtypeStruct((rows, width), dtype)] * half,
        in_specs=[VMEM] * (1 + len(blocks)),
        out_specs=[VMEM] * half,
        scratch_shapes=[pltpu.VMEM((rows * len(blocks), width), BF16)],
        compiler_params=params(),
        name="forward_partial",
    )(panel, *blocks)


def split_bias(value):
    high = value.astype(BF16)
    low = (value - high.astype(F32)).astype(BF16)
    return high, low


def bias_rows(value):
    high, low = split_bias(value)
    row = lax.broadcasted_iota(jnp.int32, (BIAS_ROWS, value.shape[1]), 0)
    high, low = high.astype(F32), low.astype(F32)
    return jnp.where(row == 0, high, jnp.where(row == 1, low, 0.0)).astype(BF16)


def bias_value(rows):
    return jnp.sum(rows.astype(F32), axis=0, keepdims=True)


def split_rows(bit, whole, bias_part, keep_ref, send_ref):
    half = whole.shape[0] // 2
    mine = jnp.where(jnp.bitwise_and(lax.axis_index("row"), bit) != 0, half, 0)
    keep_ref[:half, :] = whole[pl.ds(pl.multiple_of(mine, half), half), :]
    send_ref[:half, :] = whole[pl.ds(pl.multiple_of(half - mine, half), half), :]
    keep_ref[half:, :] = bias_part
    send_ref[half:, :] = bias_part


def dense_kernel(count, weight_ref, bias_ref, grad_ref, *refs):
    parts, outs = refs[:count], refs[count:]
    hidden_ref, agg_grad_ref, keep_ref, send_ref, weights = outs
    total = parts[0][...].astype(F32)
    for part in parts[1:]:
        total = total + part[...].astype(F32)
    aggregated = total.astype(BF16)
    weight = weight_ref[...]
    pre = jnp.dot(aggregated, weight, preferred_element_type=F32) + bias_ref[...]
    gate = jax.nn.sigmoid(pre)
    hidden_ref[...] = (pre * gate).astype(BF16)
    pre_grad = (grad_ref[...].astype(F32) * (gate * (1.0 + pre * (1.0 - gate)))).astype(BF16)
    agg_grad = lax.dot_general(
        pre_grad, weight, (((1,), (1,)), ((), ())), preferred_element_type=F32
    ).astype(BF16)
    agg_grad_ref[...] = agg_grad
    weights[...] = lax.dot_general(
        aggregated, pre_grad, (((0,), (0,)), ((), ())), preferred_element_type=F32
    ).astype(BF16)
    bias_part = bias_rows(jnp.sum(pre_grad.astype(F32), axis=0, keepdims=True))

    split_rows(1, weights, bias_part, keep_ref, send_ref)


def dense(weight, bias_vector, out_grad, parts):
    width = out_grad.shape[1]
    extra = width // 2 + BIAS_ROWS
    return pl.pallas_call(
        functools.partial(dense_kernel, len(parts)),
        out_shape=[jax.ShapeDtypeStruct(out_grad.shape, BF16)] * 2
        + [jax.ShapeDtypeStruct((extra, width), BF16)] * 2,
        in_specs=[VMEM] * (3 + len(parts)),
        out_specs=[VMEM] * 4,
        scratch_shapes=[pltpu.VMEM(weight.shape, BF16)],
        compiler_params=params(),
        name="dense_stage",
    )(weight, bias_vector, out_grad, *parts)


def tree_sum(values):
    while len(values) > 1:
        values = [values[k] + values[k + 1] for k in range(0, len(values), 2)]
    return values[0]


def gradient_sums(refs, start):
    weight = tree_sum([ref[start(ref):ref.shape[0] - BIAS_ROWS, :].astype(F32) for ref in refs])
    bias = tree_sum([bias_value(ref[ref.shape[0] - BIAS_ROWS:, :]) for ref in refs])
    return weight, bias


def split_kernel(bit, left_ref, right_ref, keep_ref, send_ref, whole):
    weight, bias = gradient_sums([left_ref, right_ref], lambda ref: 0)
    whole[...] = weight.astype(BF16)
    split_rows(bit, whole, bias_rows(bias), keep_ref, send_ref)


def split_sum(bit, left, right):
    rows, width = left.shape[0] - BIAS_ROWS, left.shape[1]
    return pl.pallas_call(
        functools.partial(split_kernel, bit),
        out_shape=[jax.ShapeDtypeStruct((rows // 2 + BIAS_ROWS, width), BF16)] * 2,
        in_specs=[VMEM, VMEM],
        out_specs=[VMEM, VMEM],
        scratch_shapes=[pltpu.VMEM((rows, width), BF16)],
        compiler_params=params(),
        name="split_sum",
    )(left, right)


def sum_kernel(count, *refs):
    weight, bias = gradient_sums(refs[:count], lambda ref: 0)
    out_ref = refs[-1]
    out_ref[:-BIAS_ROWS, :] = weight.astype(BF16)
    out_ref[-BIAS_ROWS:, :] = bias_rows(bias)


def sum_shares(shares, after):
    return pl.pallas_call(
        functools.partial(sum_kernel, len(shares)),
        out_shape=jax.ShapeDtypeStruct(shares[0].shape, BF16),
        in_specs=[VMEM] * len(shares) + [ANY] * len(after),
        out_specs=VMEM,
        compiler_params=params(),
        name="sum_shares",
    )(*shares, *after)


def halve_kernel(keep_ref, sent_ref, arrived_ref, rest_ref, send_ref):
    rows, half = keep_ref.shape[0], rest_ref.shape[0]
    held = sent_ref.shape[0] - rows
    rest_ref[...] = keep_ref[:half, :] + arrived_ref[:half, :].astype(F32)
    send_ref[:half, :] = (keep_ref[half:, :] + arrived_ref[half:rows, :].astype(F32)).astype(BF16)
    send_ref[half:half + held, :] = sent_ref[rows:, :]
    send_ref[half + held:, :] = arrived_ref[rows:, :]


def halve(keep, sent, arrived):
    rows, width = keep.shape
    size = rows // 2 + 2 * (sent.shape[0] - rows)
    return pl.pallas_call(
        halve_kernel,
        out_shape=[
            jax.ShapeDtypeStruct((rows // 2, width), F32),
            jax.ShapeDtypeStruct((size, width), BF16),
        ],
        in_specs=[VMEM] * 3,
        out_specs=[VMEM, VMEM],
        compiler_params=params(),
        name="halve_terms",
    )(keep, sent, arrived)


def final_kernel(owners, keep_ref, sent_ref, arrived_ref, feature_ref, weight_ref):
    rows = keep_ref.shape[0]
    feature_ref[...] = (keep_ref[...] + arrived_ref[:rows, :].astype(F32)).astype(BF16)
    count = len(owners)
    chunk = weight_ref.shape[0] // count
    for k, d in enumerate(owners):
        device, start, bit = jnp.bitwise_xor(lax.axis_index("row"), d), 0, 1
        while bit < count:
            start += jnp.where(jnp.bitwise_and(device, bit) != 0, chunk * count // (2 * bit), 0)
            bit *= 2
        source, place = (sent_ref, k) if k < count // 2 else (arrived_ref, k - count // 2)
        value = source[rows + place * chunk:rows + (place + 1) * chunk, :].astype(F32)
        weight_ref[pl.ds(pl.multiple_of(start, chunk), chunk), :] = value


def final(owners, keep, sent, arrived):
    rows, width = keep.shape
    return pl.pallas_call(
        functools.partial(final_kernel, owners),
        out_shape=[
            jax.ShapeDtypeStruct((rows, width), BF16),
            jax.ShapeDtypeStruct((2 * (sent.shape[0] - rows), width), F32),
        ],
        in_specs=[VMEM] * 3,
        out_specs=[VMEM, VMEM],
        compiler_params=params(),
        name="final_sums",
    )(keep, sent, arrived)


def gather_terms(blocks, gathered):
    rows = blocks[0].shape[0]
    for d, block in enumerate(blocks):
        source = jnp.bitwise_xor(lax.axis_index("col"), d)
        gathered[pl.ds(pl.multiple_of(source * rows, rows), rows), :] = block[...]


def term(panel_ref, gathered, rows, d):
    target = jnp.bitwise_xor(lax.axis_index("row"), d)
    part = panel_ref[:, pl.ds(pl.multiple_of(target * rows, rows), rows)]
    return lax.dot_general(part, gathered[...], (((0,), (0,)), ((), ())), preferred_element_type=F32)


def send_kernel(count, scale, panel_ref, left_ref, right_ref, *refs):
    blocks, (send_ref, gathered) = refs[:count], refs[count:]
    rows = blocks[0].shape[0]
    gather_terms(blocks, gathered)
    weight, _ = gradient_sums([left_ref, right_ref], lambda ref: 0)
    half = send_ref.shape[0] - weight.shape[0]
    send_ref[half:, :] = (weight * scale).astype(BF16)
    for k in range(half // rows):
        send_ref[k * rows:(k + 1) * rows, :] = term(panel_ref, gathered, rows, 2 * k + 1).astype(BF16)


def backward_send(panel, blocks, left, right, half, scale):
    rows, width = blocks[0].shape
    return pl.pallas_call(
        functools.partial(send_kernel, len(blocks), scale),
        out_shape=jax.ShapeDtypeStruct((rows * half + left.shape[0] - BIAS_ROWS, width), BF16),
        in_specs=[VMEM] * (3 + len(blocks)),
        out_specs=VMEM,
        scratch_shapes=[pltpu.VMEM((rows * len(blocks), width), BF16)],
        compiler_params=params(),
        name="backward_send",
    )(panel, left, right, *blocks)


def keep_kernel(count, scale, panel_ref, left_ref, right_ref, *refs):
    blocks, (keep_ref, bias_ref, gathered) = refs[:count], refs[count:]
    rows = blocks[0].shape[0]
    gather_terms(blocks, gathered)
    bias_ref[...] = gradient_sums([left_ref, right_ref], lambda ref: 0)[1] * scale
    for k in range(keep_ref.shape[0] // rows):
        keep_ref[k * rows:(k + 1) * rows, :] = term(panel_ref, gathered, rows, 2 * k)


def backward_keep(panel, blocks, left, right, half, scale):
    rows, width = blocks[0].shape
    return pl.pallas_call(
        functools.partial(keep_kernel, len(blocks), scale),
        out_shape=[
            jax.ShapeDtypeStruct((rows * half, width), F32),
            jax.ShapeDtypeStruct((1, width), F32),
        ],
        in_specs=[VMEM] * (3 + len(blocks)),
        out_specs=[VMEM, VMEM],
        scratch_shapes=[pltpu.VMEM((rows * len(blocks), width), BF16)],
        compiler_params=params(),
        name="backward_keep",
    )(panel, left, right, *blocks)


def body(features, weight, bias_vector, out_grad, adj_tiles, tile_pos, tile_count):
    rows_dev, width = features.shape
    tile_size = adj_tiles.shape[-1]
    row_count = lax.axis_size("row")
    col_count = lax.axis_size("col")
    row_tiles = col_count * rows_dev // tile_size
    col_tiles = row_count * rows_dev // tile_size

    blocks = [features] * row_count
    for d in range(2, row_count, 2):
        blocks[d] = swapped(features, "row", d)
    blocks[1] = swapped(features, "row", 1)
    pinned = pltpu.with_memory_space_constraint(tile_pos[0], pltpu.HBM)
    panel = build_panel(pinned, tile_count, adj_tiles[0, 0], row_tiles, col_tiles)
    for d in range(2, row_count, 2):
        blocks[d + 1] = swapped(copied(blocks[d], panel), "row", 1)
    sends = forward(panel, blocks, col_count // 2, 1, BF16)
    keeps = forward(panel, blocks, col_count // 2, 0, F32)
    parts = []
    for d, keep, send in zip(peers(col_count), keeps, sends):
        arrived = swapped(send, "col", 1)
        if d:
            pair = (keep + arrived.astype(F32)).astype(BF16)
            parts.append(swapped(pair, "col", d))
        else:
            parts += [keep, arrived]
    order = peers(col_count)[:-1]
    hidden_out, agg_grad, share, send = dense(
        weight, bias_vector.reshape(1, width), out_grad, parts
    )
    arrived = swapped(send, "row", 1)
    grads = {0: agg_grad}
    for d in order:
        grads[d] = swapped(agg_grad, "col", d)
    bit = 2
    while bit < row_count:
        share, send = split_sum(bit, share, arrived)
        arrived = swapped(send, "row", bit)
        bit *= 2
    grads[1] = swapped(agg_grad, "col", 1)
    for d in order:
        grads[d + 1] = swapped(grads[d], "col", 1)
    blocks = [grads[d] for d in range(col_count)]
    share = sum_shares([share, arrived], [grads[order[0]]])
    shares = {d: swapped(share, "col", d) for d in order}
    shares = [share] + [shares[d] for d in range(2, col_count, 2)]
    share = sum_shares(shares, [grads[1]])
    arrived = swapped(share, "col", 1)

    scale = 1.0 / math.sqrt(row_count * col_count * rows_dev)
    pair = (share, arrived, row_count // 2, scale)
    sent = backward_send(panel, blocks, *pair)
    keep, bias_grad = backward_keep(panel, blocks, *pair)
    terms = swapped(sent, "row", 1)
    owners, bit = [0, 1], row_count // 2
    while bit > 1:
        keep, sent = halve(keep, sent, terms)
        terms = swapped(sent, "row", bit)
        owners = owners + [d ^ bit for d in owners]
        bit //= 2
    feature_grad, weight_grad = final(owners, keep, sent, terms)
    return (hidden_out, feature_grad, weight_grad, bias_grad.reshape(width))


def solution(mesh):
    in_specs = (
        P(("row", "col"), None),
        P(),
        P(),
        P(("row", "col"), None),
        P("row", "col", None, None, None),
        P("row", "col", None),
        P("row", "col"),
    )
    out_specs = (P(("row", "col"), None), P(("row", "col"), None), P(), P())
    return jax.shard_map(body, mesh=mesh, in_specs=in_specs, out_specs=out_specs, check_vma=False)
```

```python
import functools
import math

import jax
import jax.numpy as jnp
from jax import lax
from jax.experimental import pallas as pl
from jax.experimental.pallas import tpu as pltpu
from jax.sharding import PartitionSpec as P

BF16 = jnp.bfloat16
F32 = jnp.float32
CHUNK = 8
BIAS_ROWS = 16
VMEM = pl.BlockSpec(memory_space=pltpu.VMEM)
ANY = pl.BlockSpec(memory_space=pl.ANY)
SMEM = pl.BlockSpec(memory_space=pltpu.SMEM)


def swapped(block, axis, bit):
    n = lax.axis_size(axis)
    return lax.ppermute(block, axis, [(i, i ^ bit) for i in range(n)])


def params(mib=32):
    return pltpu.CompilerParams(vmem_limit_bytes=mib * 1024 * 1024)


def build_kernel(col_tiles, pos_ref, count_ref, tiles_ref, panel_ref, stage, acc, places, live, sems):
    slots = tiles_ref.shape[0]
    size = tiles_ref.shape[1]
    chunks = slots // CHUNK
    copies = [
        pltpu.make_async_copy(pos_ref, places, sems.at[chunks]),
        pltpu.make_async_copy(count_ref, live, sems.at[chunks + 1]),
    ]
    for chunk in range(chunks):
        part = pl.ds(chunk * CHUNK, CHUNK)
        copies.append(pltpu.make_async_copy(tiles_ref.at[part], stage.at[part], sems.at[chunk]))
    for copy in copies:
        copy.start()
    acc[...] = jnp.zeros_like(acc)
    copies[0].wait()
    copies[1].wait()
    count = live[0, 0]

    def add(slot, carry):
        acc[places[0, slot]] += stage[slot].astype(F32)
        return carry

    for chunk in range(chunks):
        copies[chunk + 2].wait()
        lax.fori_loop(chunk * CHUNK, jnp.minimum(count, (chunk + 1) * CHUNK), add, 0)
    for place in range(acc.shape[0]):
        r, c = place // col_tiles, place % col_tiles
        panel_ref[r * size:(r + 1) * size, c * size:(c + 1) * size] = acc[place].astype(BF16)


def build_panel(positions, count, tiles, row_tiles, col_tiles):
    slots, size = tiles.shape[0], tiles.shape[1]
    places = row_tiles * col_tiles
    return pl.pallas_call(
        functools.partial(build_kernel, col_tiles),
        out_shape=jax.ShapeDtypeStruct((row_tiles * size, col_tiles * size), BF16),
        in_specs=[pl.BlockSpec(memory_space=pltpu.HBM)] * 3,
        out_specs=VMEM,
        scratch_shapes=[
            pltpu.VMEM((slots, size, size), BF16),
            pltpu.VMEM((places, size, size), F32),
            pltpu.SMEM((1, slots), jnp.int32),
            pltpu.SMEM((1, 1), jnp.int32),
            pltpu.SemaphoreType.DMA((slots // CHUNK + 2,)),
        ],
        compiler_params=params(max(52, (slots * 2 + places * 6) * size * size // 2**20 + 4)),
        cost_estimate=pl.CostEstimate(
            flops=slots * size * size, bytes_accessed=2 * slots * size * size, transcendentals=0
        ),
        name="build_panel",
    )(positions, count, tiles)


def peers(count):
    return sorted(range(2, count, 2), key=lambda d: (abs(d - count // 2 - 1.5), d)) + [0]


def copy_kernel(block_ref, after_ref, out_ref):
    out_ref[...] = block_ref[...]


def copied(block, after):
    return pl.pallas_call(
        copy_kernel,
        out_shape=jax.ShapeDtypeStruct(block.shape, block.dtype),
        in_specs=[VMEM, ANY],
        out_specs=VMEM,
        compiler_params=params(),
        name="copy_block",
    )(block, after)


def forward_kernel(count, flip, panel_ref, *refs):
    blocks, outs, gathered = refs[:count], refs[count:-1], refs[-1]
    rows = blocks[0].shape[0]
    row_me, col_me = lax.axis_index("row"), lax.axis_index("col")
    for d in range(count):
        source = jnp.bitwise_xor(row_me, d)
        gathered[pl.ds(pl.multiple_of(source * rows, rows), rows), :] = blocks[d][...]
    for d, out in zip(peers(2 * len(outs)), outs):
        target = jnp.bitwise_xor(col_me, d + flip)
        part = panel_ref[pl.ds(pl.multiple_of(target * rows, rows), rows), :]
        out[...] = jnp.dot(part, gathered[...], preferred_element_type=F32).astype(out.dtype)


def forward(panel, blocks, half, flip, dtype):
    rows, width = blocks[0].shape
    return pl.pallas_call(
        functools.partial(forward_kernel, len(blocks), flip),
        out_shape=[jax.ShapeDtypeStruct((rows, width), dtype)] * half,
        in_specs=[VMEM] * (1 + len(blocks)),
        out_specs=[VMEM] * half,
        scratch_shapes=[pltpu.VMEM((rows * len(blocks), width), BF16)],
        compiler_params=params(),
        name="forward_partial",
    )(panel, *blocks)


def split_bias(value):
    high = value.astype(BF16)
    low = (value - high.astype(F32)).astype(BF16)
    return high, low


def bias_rows(value):
    high, low = split_bias(value)
    row = lax.broadcasted_iota(jnp.int32, (BIAS_ROWS, value.shape[1]), 0)
    high, low = high.astype(F32), low.astype(F32)
    return jnp.where(row == 0, high, jnp.where(row == 1, low, 0.0)).astype(BF16)


def bias_value(rows):
    return jnp.sum(rows.astype(F32), axis=0, keepdims=True)


def split_rows(bit, whole, bias_part, keep_ref, send_ref):
    half = whole.shape[0] // 2
    mine = jnp.where(jnp.bitwise_and(lax.axis_index("row"), bit) != 0, half, 0)
    keep_ref[:half, :] = whole[pl.ds(pl.multiple_of(mine, half), half), :]
    send_ref[:half, :] = whole[pl.ds(pl.multiple_of(half - mine, half), half), :]
    keep_ref[half:, :] = bias_part
    send_ref[half:, :] = bias_part


def dense_kernel(count, weight_ref, bias_ref, grad_ref, *refs):
    parts, outs = refs[:count], refs[count:]
    hidden_ref, agg_grad_ref, keep_ref, send_ref, weights = outs
    total = parts[0][...].astype(F32)
    for part in parts[1:]:
        total = total + part[...].astype(F32)
    aggregated = total.astype(BF16)
    weight = weight_ref[...]
    pre = jnp.dot(aggregated, weight, preferred_element_type=F32) + bias_ref[...]
    gate = jax.nn.sigmoid(pre)
    hidden_ref[...] = (pre * gate).astype(BF16)
    pre_grad = (grad_ref[...].astype(F32) * (gate * (1.0 + pre * (1.0 - gate)))).astype(BF16)
    agg_grad = lax.dot_general(
        pre_grad, weight, (((1,), (1,)), ((), ())), preferred_element_type=F32
    ).astype(BF16)
    agg_grad_ref[...] = agg_grad
    weights[...] = lax.dot_general(
        aggregated, pre_grad, (((0,), (0,)), ((), ())), preferred_element_type=F32
    ).astype(BF16)
    bias_part = bias_rows(jnp.sum(pre_grad.astype(F32), axis=0, keepdims=True))

    split_rows(1, weights, bias_part, keep_ref, send_ref)


def dense(weight, bias_vector, out_grad, parts):
    width = out_grad.shape[1]
    extra = width // 2 + BIAS_ROWS
    return pl.pallas_call(
        functools.partial(dense_kernel, len(parts)),
        out_shape=[jax.ShapeDtypeStruct(out_grad.shape, BF16)] * 2
        + [jax.ShapeDtypeStruct((extra, width), BF16)] * 2,
        in_specs=[VMEM] * (3 + len(parts)),
        out_specs=[VMEM] * 4,
        scratch_shapes=[pltpu.VMEM(weight.shape, BF16)],
        compiler_params=params(),
        name="dense_stage",
    )(weight, bias_vector, out_grad, *parts)


def tree_sum(values):
    while len(values) > 1:
        values = [values[k] + values[k + 1] for k in range(0, len(values), 2)]
    return values[0]


def gradient_sums(refs, start):
    weight = tree_sum([ref[start(ref):ref.shape[0] - BIAS_ROWS, :].astype(F32) for ref in refs])
    bias = tree_sum([bias_value(ref[ref.shape[0] - BIAS_ROWS:, :]) for ref in refs])
    return weight, bias


def split_kernel(bit, left_ref, right_ref, keep_ref, send_ref, whole):
    weight, bias = gradient_sums([left_ref, right_ref], lambda ref: 0)
    whole[...] = weight.astype(BF16)
    split_rows(bit, whole, bias_rows(bias), keep_ref, send_ref)


def split_sum(bit, left, right):
    rows, width = left.shape[0] - BIAS_ROWS, left.shape[1]
    return pl.pallas_call(
        functools.partial(split_kernel, bit),
        out_shape=[jax.ShapeDtypeStruct((rows // 2 + BIAS_ROWS, width), BF16)] * 2,
        in_specs=[VMEM, VMEM],
        out_specs=[VMEM, VMEM],
        scratch_shapes=[pltpu.VMEM((rows, width), BF16)],
        compiler_params=params(),
        name="split_sum",
    )(left, right)


def sum_kernel(count, *refs):
    weight, bias = gradient_sums(refs[:count], lambda ref: 0)
    out_ref = refs[-1]
    out_ref[:-BIAS_ROWS, :] = weight.astype(BF16)
    out_ref[-BIAS_ROWS:, :] = bias_rows(bias)


def sum_shares(shares, after):
    return pl.pallas_call(
        functools.partial(sum_kernel, len(shares)),
        out_shape=jax.ShapeDtypeStruct(shares[0].shape, BF16),
        in_specs=[VMEM] * len(shares) + [ANY] * len(after),
        out_specs=VMEM,
        compiler_params=params(),
        name="sum_shares",
    )(*shares, *after)


def halve_kernel(keep_ref, sent_ref, arrived_ref, rest_ref, send_ref):
    rows, half = keep_ref.shape[0], rest_ref.shape[0]
    held = sent_ref.shape[0] - rows
    rest_ref[...] = keep_ref[:half, :] + arrived_ref[:half, :].astype(F32)
    send_ref[:half, :] = (keep_ref[half:, :] + arrived_ref[half:rows, :].astype(F32)).astype(BF16)
    send_ref[half:half + held, :] = sent_ref[rows:, :]
    send_ref[half + held:, :] = arrived_ref[rows:, :]


def halve(keep, sent, arrived):
    rows, width = keep.shape
    size = rows // 2 + 2 * (sent.shape[0] - rows)
    return pl.pallas_call(
        halve_kernel,
        out_shape=[
            jax.ShapeDtypeStruct((rows // 2, width), F32),
            jax.ShapeDtypeStruct((size, width), BF16),
        ],
        in_specs=[VMEM] * 3,
        out_specs=[VMEM, VMEM],
        compiler_params=params(),
        name="halve_terms",
    )(keep, sent, arrived)


def final_kernel(owners, keep_ref, sent_ref, arrived_ref, feature_ref, weight_ref):
    rows = keep_ref.shape[0]
    feature_ref[...] = (keep_ref[...] + arrived_ref[:rows, :].astype(F32)).astype(BF16)
    count = len(owners)
    chunk = weight_ref.shape[0] // count
    for k, d in enumerate(owners):
        device, start, bit = jnp.bitwise_xor(lax.axis_index("row"), d), 0, 1
        while bit < count:
            start += jnp.where(jnp.bitwise_and(device, bit) != 0, chunk * count // (2 * bit), 0)
            bit *= 2
        source, place = (sent_ref, k) if k < count // 2 else (arrived_ref, k - count // 2)
        value = source[rows + place * chunk:rows + (place + 1) * chunk, :].astype(F32)
        weight_ref[pl.ds(pl.multiple_of(start, chunk), chunk), :] = value


def final(owners, keep, sent, arrived):
    rows, width = keep.shape
    return pl.pallas_call(
        functools.partial(final_kernel, owners),
        out_shape=[
            jax.ShapeDtypeStruct((rows, width), BF16),
            jax.ShapeDtypeStruct((2 * (sent.shape[0] - rows), width), F32),
        ],
        in_specs=[VMEM] * 3,
        out_specs=[VMEM, VMEM],
        compiler_params=params(),
        name="final_sums",
    )(keep, sent, arrived)


def gather_terms(blocks, gathered):
    rows = blocks[0].shape[0]
    for d, block in enumerate(blocks):
        source = jnp.bitwise_xor(lax.axis_index("col"), d)
        gathered[pl.ds(pl.multiple_of(source * rows, rows), rows), :] = block[...]


def term(panel_ref, gathered, rows, d):
    target = jnp.bitwise_xor(lax.axis_index("row"), d)
    part = panel_ref[:, pl.ds(pl.multiple_of(target * rows, rows), rows)]
    return lax.dot_general(part, gathered[...], (((0,), (0,)), ((), ())), preferred_element_type=F32)


def send_kernel(count, scale, panel_ref, left_ref, right_ref, *refs):
    blocks, (send_ref, gathered) = refs[:count], refs[count:]
    rows = blocks[0].shape[0]
    gather_terms(blocks, gathered)
    weight, _ = gradient_sums([left_ref, right_ref], lambda ref: 0)
    half = send_ref.shape[0] - weight.shape[0]
    send_ref[half:, :] = (weight * scale).astype(BF16)
    for k in range(half // rows):
        send_ref[k * rows:(k + 1) * rows, :] = term(panel_ref, gathered, rows, 2 * k + 1).astype(BF16)


def backward_send(panel, blocks, left, right, half, scale):
    rows, width = blocks[0].shape
    return pl.pallas_call(
        functools.partial(send_kernel, len(blocks), scale),
        out_shape=jax.ShapeDtypeStruct((rows * half + left.shape[0] - BIAS_ROWS, width), BF16),
        in_specs=[VMEM] * (3 + len(blocks)),
        out_specs=VMEM,
        scratch_shapes=[pltpu.VMEM((rows * len(blocks), width), BF16)],
        compiler_params=params(),
        name="backward_send",
    )(panel, left, right, *blocks)


def keep_kernel(count, scale, panel_ref, left_ref, right_ref, *refs):
    blocks, (keep_ref, bias_ref, gathered) = refs[:count], refs[count:]
    rows = blocks[0].shape[0]
    gather_terms(blocks, gathered)
    bias_ref[...] = gradient_sums([left_ref, right_ref], lambda ref: 0)[1] * scale
    for k in range(keep_ref.shape[0] // rows):
        keep_ref[k * rows:(k + 1) * rows, :] = term(panel_ref, gathered, rows, 2 * k)


def backward_keep(panel, blocks, left, right, half, scale):
    rows, width = blocks[0].shape
    return pl.pallas_call(
        functools.partial(keep_kernel, len(blocks), scale),
        out_shape=[
            jax.ShapeDtypeStruct((rows * half, width), F32),
            jax.ShapeDtypeStruct((1, width), F32),
        ],
        in_specs=[VMEM] * (3 + len(blocks)),
        out_specs=[VMEM, VMEM],
        scratch_shapes=[pltpu.VMEM((rows * len(blocks), width), BF16)],
        compiler_params=params(),
        name="backward_keep",
    )(panel, left, right, *blocks)


def body(features, weight, bias_vector, out_grad, adj_tiles, tile_pos, tile_count):
    rows_dev, width = features.shape
    tile_size = adj_tiles.shape[-1]
    row_count = lax.axis_size("row")
    col_count = lax.axis_size("col")
    row_tiles = col_count * rows_dev // tile_size
    col_tiles = row_count * rows_dev // tile_size

    blocks = [features] * row_count
    for d in range(2, row_count, 2):
        blocks[d] = swapped(features, "row", d)
    blocks[1] = swapped(features, "row", 1)
    pinned = pltpu.with_memory_space_constraint(tile_pos[0], pltpu.HBM)
    panel = build_panel(pinned, tile_count, adj_tiles[0, 0], row_tiles, col_tiles)
    for d in range(2, row_count, 2):
        blocks[d + 1] = swapped(copied(blocks[d], panel), "row", 1)
    sends = forward(panel, blocks, col_count // 2, 1, BF16)
    keeps = forward(panel, blocks, col_count // 2, 0, F32)
    parts = []
    for d, keep, send in zip(peers(col_count), keeps, sends):
        arrived = swapped(send, "col", 1)
        if d:
            pair = (keep + arrived.astype(F32)).astype(BF16)
            parts.append(swapped(pair, "col", d))
        else:
            parts += [keep, arrived]
    order = peers(col_count)[:-1]
    hidden_out, agg_grad, share, send = dense(
        weight, bias_vector.reshape(1, width), out_grad, parts
    )
    arrived = swapped(send, "row", 1)
    grads = {0: agg_grad}
    for d in order:
        grads[d] = swapped(agg_grad, "col", d)
    bit = 2
    while bit < row_count:
        share, send = split_sum(bit, share, arrived)
        arrived = swapped(send, "row", bit)
        bit *= 2
    grads[1] = swapped(agg_grad, "col", 1)
    for d in order:
        grads[d + 1] = swapped(grads[d], "col", 1)
    blocks = [grads[d] for d in range(col_count)]
    share = sum_shares([share, arrived], [grads[order[0]]])
    shares = {d: swapped(share, "col", d) for d in order}
    shares = [share] + [shares[d] for d in range(2, col_count, 2)]
    share = sum_shares(shares, [grads[1]])
    arrived = swapped(share, "col", 1)

    scale = 1.0 / math.sqrt(row_count * col_count * rows_dev)
    pair = (share, arrived, row_count // 2, scale)
    sent = backward_send(panel, blocks, *pair)
    keep, bias_grad = backward_keep(panel, blocks, *pair)
    terms = swapped(sent, "row", 1)
    owners, bit = [0, 1], row_count // 2
    while bit > 1:
        keep, sent = halve(keep, sent, terms)
        terms = swapped(sent, "row", bit)
        owners = owners + [d ^ bit for d in owners]
        bit //= 2
    feature_grad, weight_grad = final(owners, keep, sent, terms)
    return (hidden_out, feature_grad, weight_grad, bias_grad.reshape(width))


def solution(mesh):
    in_specs = (
        P(("row", "col"), None),
        P(),
        P(),
        P(("row", "col"), None),
        P("row", "col", None, None, None),
        P("row", "col", None),
        P("row", "col"),
    )
    out_specs = (P(("row", "col"), None), P(("row", "col"), None), P(), P())
    return jax.shard_map(body, mesh=mesh, in_specs=in_specs, out_specs=out_specs, check_vma=False)
```
